32 devices in a mesh: pb: 8 (over z, x), vert: 4 (over y, core).
Axes of the slice: x: 2, y: 2, z: 4, core: 2. Of those that a mesh axis runs over, the one named last changes fastest.
Arguments:
- orbitals: bfloat16 [16, 32, 1024], P('pb', None, 'vert'), may hold values from -6 to 6
- transition: float32 [16, 256], P('pb'), may hold values from -0.9 to 0.9
- trial: float32 [8, 16, 256], P('vert', 'pb'), may hold values from -6 to 6
- screened: bfloat16 [16, 1024, 1024], P('pb', None, 'vert'), may hold values from -0.00030517578 to 0.00030517578
- bare: bfloat16 [1024, 1024], replicated, may hold values from -6.1035156e-05 to 6.1035156e-05
- cheb: float32 [3], replicated, may hold values from 0.5 to 1.5
- pair_k: int32 [24], P('pb'), may hold values from 0 to 15
- pair_slot: int32 [24], P('pb'), may hold values from 0 to 1
- k_order: int32 [16], replicated, may hold values from 0 to 15, each once
Outputs:
- filtered: float32 [8, 16, 256], P('vert', 'pb')
The draws below stay inside these ranges and needn't reach their ends.
Inputs may be any that keep to these rules, and one draw needn't show every extreme that they name: The pair i lies with the owner of its momentum transfer 2 * (i // 3) + pair_slot[i]. `k_order`: A permutation of the k-points.
All inputs are finite; a program needn't handle non-finite values.
Results may differ from the reference program's by a relative error of at most 0.0075.
Values may be sent and summed in bfloat16 or wider, within the bound.
A program may use at most 64 MiB of HBM per device.

```python
import math
import jax
import jax.numpy as jnp
import numpy as np
from jax import lax

NV = 16
NC = 16
NP = 1024
K_DEV = 2
NVEC = 8
PAIRS_DEV = 3
NK = 16
PAIRS = 24
NB = 32
VC = 256


def place_ends(entries, rng, smallest, high):
    dims = entries.shape
    index_at = [jax.random.randint(jax.random.fold_in(rng, axis), (), 0, dims[axis]) for axis in range(len(dims))]
    entries = entries.at[tuple(index_at)].set(smallest)
    longest = dims.index(max(dims))
    index_at[longest] = (index_at[longest] + 1) % dims[longest]
    return entries.at[tuple(index_at)].set(high)


def block_levels(stream_key, extent, split, smallest, top_value):
    level, own = 1.0, jax.random.fold_in(stream_key, 6)
    for position, blocks in split:
        steps = jnp.exp(jax.random.uniform(jax.random.fold_in(own, position), (blocks,), jnp.float32, smallest / len(split), top_value / len(split)))
        level = level * jnp.repeat(steps, extent[position] // blocks).reshape([-1 if axis == position else 1 for axis in range(len(extent))])
    return level


def rank_bounds(number_of, lean):
    portions = [(1 << 20) // math.isqrt(grade ** lean) + 1 for grade in range(1, number_of + 1)]
    spread = 1 + sum(portions) // (1 << 30)
    return np.cumsum(np.array([max(1, weight // spread) for weight in portions]))


def skewed_ids(own_key, extent, count, slope):
    listing = rank_bounds(count, slope)
    lot = jax.random.randint(jax.random.fold_in(own_key, 1), extent, 0, int(listing[count - 1]))
    standing = jnp.searchsorted(jnp.asarray(listing, jnp.int32), lot, side="right")
    return jax.random.permutation(jax.random.fold_in(own_key, 2), count)[standing].astype(jnp.int32)


def scatter_about(key, dims, spread, most, cuts=(), kind=jnp.bfloat16):
    result = jax.random.normal(key, dims, jnp.float32) * spread
    if len(cuts) > 0:
        result = block_levels(key, dims, cuts, -0.22, 0.18) * result
    return jnp.clip(result, min=-most, max=most).astype(kind)


def setup_inputs(seed: int = 0) -> dict:
    splits = jax.random.split(jax.random.key(seed), 10)
    orbitals = scatter_about(splits[0], (NK, NB, NP), 1.0, 6.0, ((0, 8), (2, 4)))
    transition = jnp.clip(jax.random.uniform(splits[1], (NK, VC), jnp.float32, -0.9, 0.9) * block_levels(splits[1], (NK, VC), ((0, 8),), -0.4, 0.0), -0.9, 0.9)
    trial = scatter_about(splits[2], (NVEC, NK, VC), 1.0, 6.0, ((0, 4), (1, 8)), jnp.float32)
    screened = scatter_about(splits[3], (NK, NP, NP), (1.0 / (48 * NP)), 0.00030517578, ((0, 8), (2, 4)))
    bare = scatter_about(splits[4], (NP, NP), (1.0 / (256 * NP)), 6.103515625e-05)
    cheb = jnp.clip(jax.random.uniform(splits[5], (3,), jnp.float32, 0.5, 1.5), 0.5, 1.5)
    pair_k = place_ends(skewed_ids(splits[6], (PAIRS,), NK, 2), jax.random.fold_in(splits[6], 3), 0, NK - 1).astype(jnp.int32)
    pair_slot = place_ends(jax.random.randint(splits[7], (PAIRS,), 0, K_DEV), jax.random.fold_in(splits[7], 1), 0, K_DEV - 1).astype(jnp.int32)
    k_order = jax.random.permutation(splits[8], NK).astype(jnp.int32)
    return {"orbitals": orbitals, "transition": transition, "trial": trial, "screened": screened, "bare": bare, "cheb": cheb, "pair_k": pair_k, "pair_slot": pair_slot, "k_order": k_order}


def reference(orbitals, transition, trial, screened, bare, cheb, pair_k, pair_slot, k_order):
    storage = jnp.zeros((NK,), jnp.int32).at[k_order].set(jnp.arange(NK, dtype=jnp.int32))
    transfer = ((jnp.arange(PAIRS, dtype=jnp.int32) // PAIRS_DEV) * K_DEV + pair_slot).astype(jnp.int32)
    partner = jnp.mod(pair_k - transfer, NK).astype(jnp.int32)
    row_first = storage[pair_k]
    row_second = storage[partner]
    pair_width = NV * NC

    def build_block(pair_index):
        orb_first = orbitals[row_first[pair_index]].astype(jnp.float32)
        orb_second = orbitals[row_second[pair_index]].astype(jnp.float32)
        left_pair = (orb_first[:NV, None, :] * orb_second[None, :NV, :]).reshape(NV * NV, NP).astype(jnp.bfloat16)
        right_pair = (orb_first[NV:, None, :] * orb_second[None, NV:, :]).reshape(NC * NC, NP).astype(jnp.bfloat16)
        half_product = jnp.dot(left_pair, screened[transfer[pair_index]], preferred_element_type=jnp.float32).astype(jnp.bfloat16)
        block_full = jnp.dot(half_product, right_pair.T, preferred_element_type=jnp.float32)
        return block_full.reshape(NV, NV, NC, NC).transpose(0, 2, 1, 3).reshape(pair_width, pair_width)

    blocks = lax.map(build_block, jnp.arange(PAIRS, dtype=jnp.int32))
    orb_all = orbitals.astype(jnp.float32)
    products = (orb_all[:, :NV, None, :] * orb_all[:, None, NV:, :]).reshape(NK, pair_width, NP).astype(jnp.bfloat16)
    hp = lax.Precision.HIGHEST

    def apply_kernel(current):
        gathered_first = current[:, row_first].astype(jnp.float32)
        gathered_second = current[:, row_second].astype(jnp.float32)
        toward_first = jnp.einsum("pij,npj->npi", blocks, gathered_second, precision=hp)
        toward_second = jnp.einsum("pij,npi->npj", blocks, gathered_first, precision=hp)
        screened_term = jnp.zeros((NVEC, NK, pair_width), jnp.float32)
        screened_term = screened_term.at[:, row_first].add(toward_first).at[:, row_second].add(toward_second)
        density = jnp.einsum("nkj,kjm->nm", current.astype(jnp.float32), products.astype(jnp.float32), precision=hp).astype(jnp.bfloat16)
        potential = jnp.dot(density, bare.T, preferred_element_type=jnp.float32).astype(jnp.bfloat16)
        bare_term = jnp.einsum("kjm,nm->nkj", products.astype(jnp.float32), potential.astype(jnp.float32), precision=hp)
        return transition[None] * current.astype(jnp.float32) + 2.0 * bare_term - screened_term

    first_step = apply_kernel(trial.astype(jnp.bfloat16))
    second_step = 2.0 * apply_kernel(first_step.astype(jnp.bfloat16)) - trial
    return cheb[0] * trial + cheb[1] * first_step + cheb[2] * second_step
```

```python
import functools

import jax
import jax.numpy as jnp
from jax import lax
from jax.experimental import pallas as pl
from jax.experimental.pallas import tpu as pltpu
from jax.sharding import PartitionSpec as P

NV = 16
LANES = 128
MESH = pl.DeviceIdType.MESH
F32 = jnp.float32
BF16 = jnp.bfloat16
TRANSPOSED = (((1,), (1,)), ((), ()))


def kernel(
    pn, vn, orb, trans, trial, scr, bare, cheb, pair_k, pair_slot, k_order, out,
    orb_all, x_all, x_own, x_tile, trial_tile, trans_tile, proj, val_own, val_all, half,
    dens_own, dens_all, bare_own, weighted, result, bare_part, part, part_all,
    bare_sem, orb_sem, val_sem, x_sem, dens_sem, part_sem,
):
    me_p, me_v = lax.axis_index("pb"), lax.axis_index("vert")
    count = pn * vn
    me = me_p * vn + me_v
    kl, bands, ml = orb.shape
    valence = NV
    cond = bands - valence
    width = valence * cond
    nl = trial.shape[0]
    nvec = nl * vn
    pairs = pair_k.shape[0]
    ktot = k_order.shape[0]
    rows = valence * nvec
    halves = width // LANES

    barrier = pltpu.get_barrier_semaphore()

    @pl.loop(1, count)
    def _(i):
        t = lax.rem(me + i, count)
        pl.semaphore_signal(barrier, inc=1, device_id=(t // vn, lax.rem(t, vn)), device_id_type=MESH)

    bare_copy = pltpu.make_async_copy(bare.at[pl.ds(pl.multiple_of(me_v * ml, ml), ml)], bare_own, bare_sem)
    bare_copy.start()
    for h in range(halves):
        for k in range(kl):
            for n in range(nl):
                at = (h * kl + k) * nl + n
                cols = slice(h * LANES, (h + 1) * LANES)
                trial_tile[at : at + 1, :] = trial[n, k : k + 1, cols]
                trans_tile[at : at + 1, :] = trans[k : k + 1, cols]
    x_own[0] = trial_tile[...]
    orb_all[pl.ds(me_p * kl, kl)] = orb[...]

    ends = []
    for p in range(pairs):
        first = pair_k[p]
        second = lax.rem(first - (me_p * kl + pair_slot[p]) + ktot, ktot)
        ends += [first, second]

    def find(r, found):
        key = k_order[r]
        return tuple(jnp.where(key == e, r, f) for e, f in zip(ends, found))

    dest = lax.fori_loop(0, ktot, find, tuple(jnp.int32(0) for _ in ends))

    pl.semaphore_wait(barrier, count - 1)

    def orb_send(i):
        return pltpu.make_async_remote_copy(
            src_ref=orb, dst_ref=orb_all.at[pl.ds(me_p * kl, kl)], send_sem=orb_sem.at[0],
            recv_sem=orb_sem.at[1], device_id=(lax.rem(me_p + i, pn), me_v), device_id_type=MESH)

    @pl.loop(1, pn)
    def _(i):
        orb_send(i).start()

    def x_send(a):
        x_all[a, me] = x_own[a]

        @pl.loop(1, count)
        def _(i):
            t = lax.rem(me + i, count)
            pltpu.make_async_remote_copy(
                src_ref=x_own.at[a], dst_ref=x_all.at[a, me], send_sem=x_sem.at[0, a],
                recv_sem=x_sem.at[1, a], device_id=(t // vn, lax.rem(t, vn)), device_id_type=MESH).start()

    def vert_send(src, dst, sems):
        @pl.loop(1, vn)
        def _(i):
            pltpu.make_async_remote_copy(
                src_ref=src, dst_ref=dst.at[me_v], send_sem=sems[0], recv_sem=sems[1],
                device_id=(me_p, lax.rem(me_v + i, vn)), device_id_type=MESH).start()

    def drain(ref, sem):
        pltpu.make_async_copy(ref, ref, sem).wait()

    x_send(0)
    drain(orb_all.at[pl.ds(0, (pn - 1) * kl)], orb_sem.at[1])
    for e in range(2 * pairs):
        val_own[e] = orb_all[dest[e], 0:valence, :]
    val_all[me_v] = val_own[...]
    vert_send(val_own, val_all, (val_sem.at[0], val_sem.at[1]))

    own_block = (
        lax.broadcasted_iota(jnp.int32, (rows, width), 0) // nvec
        == lax.broadcasted_iota(jnp.int32, (rows, width), 1) // cond
    )

    def tiled(r):
        return jnp.concatenate([orb_all[r, valence:bands, :]] * valence, axis=0)

    def back(value, r):
        spread = lax.dot_general(value.astype(BF16), tiled(r), TRANSPOSED, preferred_element_type=F32)
        spread = jnp.where(own_block, spread, 0.0)
        return jnp.sum(spread.reshape(valence, nvec, width), axis=0)

    def apply_kernel(a):
        drain(x_all.at[a, pl.ds(0, count - 1)], x_sem.at[1, a])

        def project(d, density):
            for k in range(kl):
                r = d * kl + k
                for w in range(vn):
                    for h in range(halves):
                        at = (h * kl + k) * nl
                        x_tile[w * nl : (w + 1) * nl, h * LANES : (h + 1) * LANES] = x_all[
                            a, d * vn + w, at : at + nl, :]
                wide = jnp.where(own_block, jnp.concatenate([x_tile[...]] * valence, axis=0), 0.0)
                y = jnp.dot(wide.astype(BF16), tiled(r), preferred_element_type=F32)
                proj[r] = y
                vals = orb_all[r, 0:valence, :].astype(F32)
                for v in range(valence):
                    density = density + y[v * nvec : (v + 1) * nvec] * vals[v : v + 1]
            return density

        density = lax.fori_loop(0, pn, project, jnp.zeros((nvec, ml), F32))
        dens_own[a] = density
        dens_all[a, me_v] = density
        vert_send(dens_own.at[a], dens_all.at[a], (dens_sem.at[0, a], dens_sem.at[1, a]))

        if a == 0:
            drain(val_all.at[pl.ds(0, vn - 1)], val_sem.at[1])
            for p in range(pairs):
                def add(w, total, p=p):
                    one = val_all[w, 2 * p].astype(F32)
                    two = val_all[w, 2 * p + 1].astype(F32)
                    left = jnp.concatenate(
                        [(one[v : v + 1] * two).astype(BF16) for v in range(valence)], axis=0)
                    matrix = scr[pair_slot[p], pl.ds(pl.multiple_of(w * ml, ml), ml), :]
                    return total + jnp.dot(left, matrix, preferred_element_type=F32)

                total = lax.fori_loop(0, vn, add, jnp.zeros((valence * valence, ml), F32))
                half[p] = total.astype(BF16).astype(F32).reshape(valence, valence, ml)

        for p in range(pairs):
            @pl.loop(0, valence)
            def _(v, p=p):
                total = jnp.zeros((nvec, ml), F32)
                other = jnp.zeros((nvec, ml), F32)
                line = half[p, v]
                for u in range(valence):
                    total = total + line[u : u + 1] * proj[dest[2 * p + 1], u * nvec : (u + 1) * nvec, :]
                    other = other + half[p, u, pl.ds(v, 1), :] * proj[dest[2 * p], u * nvec : (u + 1) * nvec, :]
                here = pl.ds(pl.multiple_of(v * nvec, nvec), nvec)
                weighted[0, here] = total
                weighted[1, here] = other

            result[2 * p] = back(weighted[0], dest[2 * p])
            result[2 * p + 1] = back(weighted[1], dest[2 * p + 1])

        drain(dens_all.at[a, pl.ds(0, vn - 1)], dens_sem.at[1, a])
        if a == 0:
            bare_copy.wait()
        potential = jnp.zeros((nvec, ml), F32)
        for w in range(vn):
            potential = potential + lax.dot_general(
                dens_all[a, w].astype(BF16), bare_own[:, w * ml : (w + 1) * ml], TRANSPOSED,
                preferred_element_type=F32)
        potential = potential.astype(BF16).astype(F32)
        for k in range(kl):
            vals = orb[k, 0:valence, :].astype(F32)
            value = jnp.concatenate([vals[v : v + 1] * potential for v in range(valence)], axis=0)
            bare_part[k] = 2.0 * back(value, me_p * kl + k)

        @pl.loop(0, pn)
        def _(d):
            mine = jnp.where(d == me_p, 1.0, 0.0)
            for k in range(kl):
                total = mine * bare_part[k]
                for e in range(2 * pairs):
                    total = total - jnp.where(dest[e] == d * kl + k, 1.0, 0.0) * result[e]
                for w in range(vn):
                    for h in range(halves):
                        at = (h * kl + k) * nl
                        part[a, d * vn + w, at : at + nl, :] = total[
                            w * nl : (w + 1) * nl, h * LANES : (h + 1) * LANES]

        part_all[a, me] = part[a, me]

        @pl.loop(1, count)
        def _(i):
            t = lax.rem(me + i, count)
            pltpu.make_async_remote_copy(
                src_ref=part.at[a, t], dst_ref=part_all.at[a, me], send_sem=part_sem.at[0, a],
                recv_sem=part_sem.at[1, a], device_id=(t // vn, lax.rem(t, vn)), device_id_type=MESH).start()

        drain(part_all.at[a, pl.ds(0, count - 1)], part_sem.at[1, a])
        total = jnp.sum(part_all[a], axis=0)
        current = x_own[a].astype(BF16).astype(F32)
        return trans_tile[...] * current + total

    first_step = apply_kernel(0)
    x_own[1] = first_step
    x_send(1)
    second_step = 2.0 * apply_kernel(1) - trial_tile[...]
    filtered = cheb[0] * trial_tile[...] + cheb[1] * x_own[1] + cheb[2] * second_step
    for h in range(halves):
        for k in range(kl):
            for n in range(nl):
                at = (h * kl + k) * nl + n
                out[n, k : k + 1, h * LANES : (h + 1) * LANES] = filtered[at : at + 1]

    drain(orb_all.at[pl.ds(0, (pn - 1) * kl)], orb_sem.at[0])
    drain(val_all.at[pl.ds(0, vn - 1)], val_sem.at[0])
    for a in range(2):
        drain(x_all.at[a, pl.ds(0, count - 1)], x_sem.at[0, a])
        drain(dens_all.at[a, pl.ds(0, vn - 1)], dens_sem.at[0, a])
        drain(part_all.at[a, pl.ds(0, count - 1)], part_sem.at[0, a])


def body(pn, vn, orbitals, transition, trial, screened, bare, cheb, pair_k, pair_slot, k_order):
    kl, bands, ml = orbitals.shape
    nl, _, width = trial.shape
    pairs = pair_k.shape[0]
    ktot = k_order.shape[0]
    nvec = nl * vn
    count = pn * vn
    tile = (nl * kl * width // LANES, LANES)
    vmem = pl.BlockSpec(memory_space=pltpu.VMEM)
    smem = pl.BlockSpec(memory_space=pltpu.SMEM)
    dma = pltpu.SemaphoreType.DMA
    return pl.pallas_call(
        functools.partial(kernel, pn, vn),
        out_shape=jax.ShapeDtypeStruct(trial.shape, F32),
        in_specs=[vmem, vmem, vmem, vmem, pl.BlockSpec(memory_space=pl.ANY), smem, smem, smem, smem],
        out_specs=vmem,
        scratch_shapes=[
            pltpu.VMEM((ktot, bands, ml), BF16),
            pltpu.VMEM((2, count) + tile, F32),
            pltpu.VMEM((2,) + tile, F32),
            pltpu.VMEM((nvec, width), F32),
            pltpu.VMEM(tile, F32),
            pltpu.VMEM(tile, F32),
            pltpu.VMEM((ktot, NV * nvec, ml), F32),
            pltpu.VMEM((2 * pairs, NV, ml), BF16),
            pltpu.VMEM((vn, 2 * pairs, NV, ml), BF16),
            pltpu.VMEM((pairs, NV, NV, ml), F32),
            pltpu.VMEM((2, nvec, ml), F32),
            pltpu.VMEM((2, vn, nvec, ml), F32),
            pltpu.VMEM((ml, vn * ml), BF16),
            pltpu.VMEM((2, NV * nvec, ml), F32),
            pltpu.VMEM((2 * pairs, nvec, width), F32),
            pltpu.VMEM((kl, nvec, width), F32),
            pltpu.VMEM((2, count) + tile, F32),
            pltpu.VMEM((2, count) + tile, F32),
            dma, dma((2,)), dma((2,)), dma((2, 2)), dma((2, 2)), dma((2, 2)),
        ],
        compiler_params=pltpu.CompilerParams(
            collective_id=0, has_side_effects=True, vmem_limit_bytes=56 * 2**20),
    )(orbitals, transition, trial, screened, bare, cheb, pair_k, pair_slot, k_order)


def solution(mesh):
    in_specs = (
        P("pb", None, "vert"),
        P("pb", None),
        P("vert", "pb", None),
        P("pb", None, "vert"),
        P(),
        P(),
        P("pb"),
        P("pb"),
        P(),
    )
    out_specs = P("vert", "pb", None)
    step = functools.partial(body, mesh.shape["pb"], mesh.shape["vert"])
    return jax.shard_map(step, mesh=mesh, in_specs=in_specs, out_specs=out_specs, check_vma=False)
```

```python
import functools

import jax
import jax.numpy as jnp
from jax import lax
from jax.experimental import pallas as pl
from jax.experimental.pallas import tpu as pltpu
from jax.sharding import PartitionSpec as P

NV = 16
LANES = 128
MESH = pl.DeviceIdType.MESH
F32 = jnp.float32
BF16 = jnp.bfloat16
TRANSPOSED = (((1,), (1,)), ((), ()))


def kernel(
    pn, vn, orb, trans, trial, scr, bare, cheb, pair_k, pair_slot, k_order, out,
    orb_all, x_all, x_own, x_tile, trial_tile, trans_tile, proj, val_own, val_all, left, half,
    dens_own, dens_all, bare_own, weighted, result, bare_part, part, part_all,
    bare_sem, orb_sem, orb_recv, val_sem, x_sem, dens_sem, part_sem,
):
    me_p, me_v = lax.axis_index("pb"), lax.axis_index("vert")
    count = pn * vn
    me = me_p * vn + me_v
    kl, bands, ml = orb.shape
    valence = NV
    cond = bands - valence
    width = valence * cond
    nl = trial.shape[0]
    nvec = nl * vn
    pairs = pair_k.shape[0]
    ktot = k_order.shape[0]
    rows = valence * nvec
    halves = width // LANES

    barrier = pltpu.get_barrier_semaphore()

    @pl.loop(1, count)
    def _(i):
        t = lax.rem(me + i, count)
        pl.semaphore_signal(barrier, inc=1, device_id=(t // vn, lax.rem(t, vn)), device_id_type=MESH)

    bare_copy = pltpu.make_async_copy(bare.at[pl.ds(pl.multiple_of(me_v * ml, ml), ml)], bare_own, bare_sem)
    bare_copy.start()
    for h in range(halves):
        for k in range(kl):
            for n in range(nl):
                at = (h * kl + k) * nl + n
                cols = slice(h * LANES, (h + 1) * LANES)
                trial_tile[at : at + 1, :] = trial[n, k : k + 1, cols]
                trans_tile[at : at + 1, :] = trans[k : k + 1, cols]
    x_own[0] = trial_tile[...]
    orb_all[pl.ds(me_p * kl, kl)] = orb[...]

    ends = []
    for p in range(pairs):
        first = pair_k[p]
        second = lax.rem(first - (me_p * kl + pair_slot[p]) + ktot, ktot)
        ends += [first, second]

    def find(r, found):
        key = k_order[r]
        return tuple(jnp.where(key == e, r, f) for e, f in zip(ends, found))

    dest = lax.fori_loop(0, ktot, find, tuple(jnp.int32(0) for _ in ends))

    pl.semaphore_wait(barrier, count - 1)

    def drain(ref, sem):
        pltpu.make_async_copy(ref, ref, sem).wait()

    partner = me_p + 1 - 2 * lax.rem(me_p, 2)

    def orb_send(block, src, to):
        pltpu.make_async_remote_copy(
            src_ref=src, dst_ref=orb_all.at[pl.ds(block * kl, kl)], send_sem=orb_sem,
            recv_sem=orb_recv.at[block], device_id=(to, me_v), device_id_type=MESH).start()

    def orb_wait(block):
        here = orb_all.at[pl.ds(block * kl, kl)]
        drain(here, orb_recv.at[block])

    @pl.loop(1, pn // 2)
    def _(i):
        orb_send(me_p, orb, lax.rem(me_p + 2 * i, pn))

    orb_send(me_p, orb, partner)

    def x_send(a):
        x_all[a, me] = x_own[a]

        @pl.loop(1, count)
        def _(i):
            t = lax.rem(me + i, count)
            pltpu.make_async_remote_copy(
                src_ref=x_own.at[a], dst_ref=x_all.at[a, me], send_sem=x_sem.at[0, a],
                recv_sem=x_sem.at[1, a], device_id=(t // vn, lax.rem(t, vn)), device_id_type=MESH).start()

    def vert_send(src, dst, sems):
        @pl.loop(1, vn)
        def _(i):
            pltpu.make_async_remote_copy(
                src_ref=src, dst_ref=dst.at[me_v], send_sem=sems[0], recv_sem=sems[1],
                device_id=(me_p, lax.rem(me_v + i, vn)), device_id_type=MESH).start()

    x_send(0)

    @pl.loop(1, pn // 2)
    def _(i):
        block = lax.rem(me_p + pn - 2 * i, pn)
        orb_wait(block)
        orb_send(block, orb_all.at[pl.ds(block * kl, kl)], partner)

    own_block = (
        lax.broadcasted_iota(jnp.int32, (rows, width), 0) // nvec
        == lax.broadcasted_iota(jnp.int32, (rows, width), 1) // cond
    )

    def tiled(r):
        return jnp.concatenate([orb_all[r, valence:bands, :]] * valence, axis=0)

    def back(value, r):
        spread = lax.dot_general(value.astype(BF16), tiled(r), TRANSPOSED, preferred_element_type=F32)
        spread = jnp.where(own_block, spread, 0.0)
        return jnp.sum(spread.reshape(valence, nvec, width), axis=0)

    def apply_kernel(a):
        drain(x_all.at[a, pl.ds(0, count - 1)], x_sem.at[1, a])

        def project(d, density):
            for k in range(kl):
                r = d * kl + k
                for w in range(vn):
                    for h in range(halves):
                        at = (h * kl + k) * nl
                        x_tile[w * nl : (w + 1) * nl, h * LANES : (h + 1) * LANES] = x_all[
                            a, d * vn + w, at : at + nl, :]
                wide = jnp.where(own_block, jnp.concatenate([x_tile[...]] * valence, axis=0), 0.0)
                y = jnp.dot(wide.astype(BF16), tiled(r), preferred_element_type=F32)
                proj[r] = y
                vals = orb_all[r, 0:valence, :].astype(F32)
                for v in range(valence):
                    density = density + y[v * nvec : (v + 1) * nvec] * vals[v : v + 1]
            return density

        density = lax.fori_loop(
            0, pn // 2, lambda i, t: project(lax.rem(me_p + pn - 2 * i, pn), t), jnp.zeros((nvec, ml), F32))
        if a == 0:
            @pl.loop(0, pn // 2)
            def _(i):
                orb_wait(lax.rem(partner + pn - 2 * i, pn))

            for e in range(2 * pairs):
                val_own[e] = orb_all[dest[e], 0:valence, :]
            val_all[me_v] = val_own[...]
            vert_send(val_own, val_all, (val_sem.at[0], val_sem.at[1]))
        density = lax.fori_loop(
            0, pn // 2, lambda i, t: project(lax.rem(partner + pn - 2 * i, pn), t), density)
        dens_own[a] = density
        dens_all[a, me_v] = density
        vert_send(dens_own.at[a], dens_all.at[a], (dens_sem.at[0, a], dens_sem.at[1, a]))

        if a == 0:
            drain(val_all.at[pl.ds(0, vn - 1)], val_sem.at[1])
            for p in range(pairs):
                for w in range(vn):
                    one = val_all[w, 2 * p].astype(F32)
                    two = val_all[w, 2 * p + 1].astype(F32)
                    for v in range(valence):
                        left[p, v * valence : (v + 1) * valence, w * ml : (w + 1) * ml] = (
                            one[v : v + 1] * two).astype(BF16)
                total = jnp.dot(left[p], scr[pair_slot[p]], preferred_element_type=F32)
                half[p] = total.astype(BF16).astype(F32).reshape(valence, valence, ml)

        for p in range(pairs):
            for h in range(ml // LANES):
                cols = slice(h * LANES, (h + 1) * LANES)
                ahead = [proj[dest[2 * p + 1], u * nvec : (u + 1) * nvec, cols] for u in range(valence)]

                def contract(v, other, p=p, cols=cols, ahead=ahead):
                    here = pl.ds(pl.multiple_of(v * nvec, nvec), nvec)
                    line = half[p, v, :, cols]
                    mine = proj[dest[2 * p], here, cols]
                    sums, kept = [], []
                    for u in range(valence):
                        spread = jnp.broadcast_to(line[u : u + 1], (nvec, LANES))
                        sums.append(spread * ahead[u])
                        kept.append(other[u] + spread * mine)
                    while len(sums) > 1:
                        sums = [sum(sums[i : i + 2]) for i in range(0, len(sums), 2)]
                    weighted[2 * p, here, cols] = sums[0]
                    return tuple(kept)

                zero = jnp.zeros((nvec, LANES), F32)
                other = lax.fori_loop(0, valence, contract, (zero,) * valence)
                for u in range(valence):
                    weighted[2 * p + 1, u * nvec : (u + 1) * nvec, cols] = other[u]

        for e in range(2 * pairs):
            result[e] = back(weighted[e], dest[e])

        def assemble(d, own):
            for k in range(kl):
                total = bare_part[k] if own else jnp.zeros((nvec, width), F32)
                for e in range(2 * pairs):
                    total = total - jnp.where(dest[e] == d * kl + k, 1.0, 0.0) * result[e]
                for w in range(vn):
                    for h in range(halves):
                        at = (h * kl + k) * nl
                        part[a, d * vn + w, at : at + nl, :] = total[
                            w * nl : (w + 1) * nl, h * LANES : (h + 1) * LANES]

        def part_send(d, w):
            pltpu.make_async_remote_copy(
                src_ref=part.at[a, d * vn + w], dst_ref=part_all.at[a, me], send_sem=part_sem.at[0, a],
                recv_sem=part_sem.at[1, a], device_id=(d, w), device_id_type=MESH).start()

        @pl.loop(1, pn)
        def _(i):
            d = lax.rem(me_p + i, pn)
            assemble(d, False)

            @pl.loop(0, vn)
            def _(w):
                part_send(d, lax.rem(me_v + w, vn))

        drain(dens_all.at[a, pl.ds(0, vn - 1)], dens_sem.at[1, a])
        if a == 0:
            bare_copy.wait()
        potential = jnp.zeros((nvec, ml), F32)
        for w in range(vn):
            potential = potential + lax.dot_general(
                dens_all[a, w].astype(BF16), bare_own[:, w * ml : (w + 1) * ml], TRANSPOSED,
                preferred_element_type=F32)
        potential = potential.astype(BF16).astype(F32)
        for k in range(kl):
            vals = orb[k, 0:valence, :].astype(F32)
            value = jnp.concatenate([vals[v : v + 1] * potential for v in range(valence)], axis=0)
            bare_part[k] = 2.0 * back(value, me_p * kl + k)
        assemble(me_p, True)

        @pl.loop(1, vn)
        def _(w):
            part_send(me_p, lax.rem(me_v + w, vn))

        part_all[a, me] = part[a, me]
        drain(part_all.at[a, pl.ds(0, count - 1)], part_sem.at[1, a])
        total = jnp.sum(part_all[a], axis=0)
        current = x_own[a].astype(BF16).astype(F32)
        return trans_tile[...] * current + total

    first_step = apply_kernel(0)
    x_own[1] = first_step
    x_send(1)
    second_step = 2.0 * apply_kernel(1) - trial_tile[...]
    filtered = cheb[0] * trial_tile[...] + cheb[1] * x_own[1] + cheb[2] * second_step
    for h in range(halves):
        for k in range(kl):
            for n in range(nl):
                at = (h * kl + k) * nl + n
                out[n, k : k + 1, h * LANES : (h + 1) * LANES] = filtered[at : at + 1]

    drain(orb_all.at[pl.ds(0, (pn - 1) * kl)], orb_sem)
    drain(val_all.at[pl.ds(0, vn - 1)], val_sem.at[0])
    for a in range(2):
        drain(x_all.at[a, pl.ds(0, count - 1)], x_sem.at[0, a])
        drain(dens_all.at[a, pl.ds(0, vn - 1)], dens_sem.at[0, a])
        drain(part_all.at[a, pl.ds(0, count - 1)], part_sem.at[0, a])


def body(pn, vn, orbitals, transition, trial, screened, bare, cheb, pair_k, pair_slot, k_order):
    kl, bands, ml = orbitals.shape
    nl, _, width = trial.shape
    pairs = pair_k.shape[0]
    ktot = k_order.shape[0]
    nvec = nl * vn
    count = pn * vn
    tile = (nl * kl * width // LANES, LANES)
    vmem = pl.BlockSpec(memory_space=pltpu.VMEM)
    smem = pl.BlockSpec(memory_space=pltpu.SMEM)
    dma = pltpu.SemaphoreType.DMA
    return pl.pallas_call(
        functools.partial(kernel, pn, vn),
        out_shape=jax.ShapeDtypeStruct(trial.shape, F32),
        in_specs=[vmem, vmem, vmem, vmem, pl.BlockSpec(memory_space=pl.ANY), smem, smem, smem, smem],
        out_specs=vmem,
        scratch_shapes=[
            pltpu.VMEM((ktot, bands, ml), BF16),
            pltpu.VMEM((2, count) + tile, F32),
            pltpu.VMEM((2,) + tile, F32),
            pltpu.VMEM((nvec, width), F32),
            pltpu.VMEM(tile, F32),
            pltpu.VMEM(tile, F32),
            pltpu.VMEM((ktot, NV * nvec, ml), F32),
            pltpu.VMEM((2 * pairs, NV, ml), BF16),
            pltpu.VMEM((vn, 2 * pairs, NV, ml), BF16),
            pltpu.VMEM((pairs, NV * NV, vn * ml), BF16),
            pltpu.VMEM((pairs, NV, NV, ml), F32),
            pltpu.VMEM((2, nvec, ml), F32),
            pltpu.VMEM((2, vn, nvec, ml), F32),
            pltpu.VMEM((ml, vn * ml), BF16),
            pltpu.VMEM((2 * pairs, NV * nvec, ml), F32),
            pltpu.VMEM((2 * pairs, nvec, width), F32),
            pltpu.VMEM((kl, nvec, width), F32),
            pltpu.VMEM((2, count) + tile, F32),
            pltpu.VMEM((2, count) + tile, F32),
            dma, dma, dma((pn,)), dma((2,)), dma((2, 2)), dma((2, 2)), dma((2, 2)),
        ],
        compiler_params=pltpu.CompilerParams(
            collective_id=0, has_side_effects=True, vmem_limit_bytes=56 * 2**20),
    )(orbitals, transition, trial, screened, bare, cheb, pair_k, pair_slot, k_order)


def solution(mesh):
    in_specs = (
        P("pb", None, "vert"),
        P("pb", None),
        P("vert", "pb", None),
        P("pb", None, "vert"),
        P(),
        P(),
        P("pb"),
        P("pb"),
        P(),
    )
    out_specs = P("vert", "pb", None)
    step = functools.partial(body, mesh.shape["pb"], mesh.shape["vert"])
    return jax.shard_map(step, mesh=mesh, in_specs=in_specs, out_specs=out_specs, check_vma=False)
```

```python
import functools

import jax
import jax.numpy as jnp
from jax import lax
from jax.experimental import pallas as pl
from jax.experimental.pallas import tpu as pltpu
from jax.sharding import PartitionSpec as P

NV = 16
LANES = 128
MESH = pl.DeviceIdType.MESH
F32 = jnp.float32
BF16 = jnp.bfloat16
TRANSPOSED = (((1,), (1,)), ((), ()))


def kernel(
    pn, vn, orb, trans, trial, scr_hbm, bare, cheb, pair_k, pair_slot, k_order, out,
    orb_all, x_all, x_own, x_tile, trial_tile, trans_tile, proj, val_own, val_all, left, half, scr,
    dens_own, dens_all, bare_own, weighted, result, bare_part, part, part_all,
    scr_sem, bare_sem, orb_sem, orb_recv, val_sem, x_sem, dens_sem, part_sem,
):
    me_p, me_v = lax.axis_index("pb"), lax.axis_index("vert")
    count = pn * vn
    me = me_p * vn + me_v
    kl, bands, ml = orb.shape
    valence = NV
    cond = bands - valence
    width = valence * cond
    nl = trial.shape[0]
    nvec = nl * vn
    pairs = pair_k.shape[0]
    ktot = k_order.shape[0]
    rows = valence * nvec
    halves = width // LANES

    barrier = pltpu.get_barrier_semaphore()

    @pl.loop(1, count)
    def _(i):
        t = lax.rem(me + i, count)
        pl.semaphore_signal(barrier, inc=1, device_id=(t // vn, lax.rem(t, vn)), device_id_type=MESH)

    bare_copy = pltpu.make_async_copy(bare.at[pl.ds(pl.multiple_of(me_v * ml, ml), ml)], bare_own, bare_sem)
    bare_copy.start()
    scr_copy = pltpu.make_async_copy(scr_hbm, scr, scr_sem)
    scr_copy.start()
    for h in range(halves):
        for k in range(kl):
            for n in range(nl):
                at = (h * kl + k) * nl + n
                cols = slice(h * LANES, (h + 1) * LANES)
                trial_tile[at : at + 1, :] = trial[n, k : k + 1, cols]
                trans_tile[at : at + 1, :] = trans[k : k + 1, cols]
    x_own[0] = trial_tile[...]
    orb_all[pl.ds(me_p * kl, kl)] = orb[...]

    ends = []
    for p in range(pairs):
        first = pair_k[p]
        second = lax.rem(first - (me_p * kl + pair_slot[p]) + ktot, ktot)
        ends += [first, second]

    def find(r, found):
        key = k_order[r]
        return tuple(jnp.where(key == e, r, f) for e, f in zip(ends, found))

    dest = lax.fori_loop(0, ktot, find, tuple(jnp.int32(0) for _ in ends))

    pl.semaphore_wait(barrier, count - 1)

    def drain(ref, sem):
        pltpu.make_async_copy(ref, ref, sem).wait()

    partner = me_p + 1 - 2 * lax.rem(me_p, 2)

    def orb_send(block, src, to):
        pltpu.make_async_remote_copy(
            src_ref=src, dst_ref=orb_all.at[pl.ds(block * kl, kl)], send_sem=orb_sem,
            recv_sem=orb_recv.at[block], device_id=(to, me_v), device_id_type=MESH).start()

    def orb_wait(block):
        here = orb_all.at[pl.ds(block * kl, kl)]
        drain(here, orb_recv.at[block])

    @pl.loop(1, pn // 2)
    def _(i):
        orb_send(me_p, orb, lax.rem(me_p + 2 * i, pn))

    orb_send(me_p, orb, partner)

    def x_send(a):
        x_all[a, me] = x_own[a]

        @pl.loop(1, count)
        def _(i):
            t = lax.rem(me + i, count)
            pltpu.make_async_remote_copy(
                src_ref=x_own.at[a], dst_ref=x_all.at[a, me], send_sem=x_sem.at[0, a],
                recv_sem=x_sem.at[1, a], device_id=(t // vn, lax.rem(t, vn)), device_id_type=MESH).start()

    def vert_send(src, dst, sems):
        @pl.loop(1, vn)
        def _(i):
            pltpu.make_async_remote_copy(
                src_ref=src, dst_ref=dst.at[me_v], send_sem=sems[0], recv_sem=sems[1],
                device_id=(me_p, lax.rem(me_v + i, vn)), device_id_type=MESH).start()

    x_send(0)

    @pl.loop(1, pn // 2)
    def _(i):
        block = lax.rem(me_p + pn - 2 * i, pn)
        orb_wait(block)
        orb_send(block, orb_all.at[pl.ds(block * kl, kl)], partner)

    own_block = (
        lax.broadcasted_iota(jnp.int32, (rows, width), 0) // nvec
        == lax.broadcasted_iota(jnp.int32, (rows, width), 1) // cond
    )

    def tiled(r):
        return jnp.concatenate([orb_all[r, valence:bands, :]] * valence, axis=0)

    def back(value, r):
        spread = lax.dot_general(value.astype(BF16), tiled(r), TRANSPOSED, preferred_element_type=F32)
        spread = jnp.where(own_block, spread, 0.0)
        return jnp.sum(spread.reshape(valence, nvec, width), axis=0)

    def apply_kernel(a):
        drain(x_all.at[a, pl.ds(0, count - 1)], x_sem.at[1, a])

        def project(d, density, turn):
            for k in range(kl):
                r = d * kl + k
                for w in range(vn):
                    for h in range(halves):
                        at = (h * kl + k) * nl
                        x_tile[turn * kl + k, w * nl : (w + 1) * nl, h * LANES : (h + 1) * LANES] = x_all[
                            a, d * vn + w, at : at + nl, :]
                wide = jnp.where(own_block, jnp.concatenate([x_tile[turn * kl + k]] * valence, axis=0), 0.0)
                y = jnp.dot(wide.astype(BF16), tiled(r), preferred_element_type=F32)
                proj[r] = y
                vals = orb_all[r, 0:valence, :].astype(F32)
                for v in range(valence):
                    density = density + y[v * nvec : (v + 1) * nvec] * vals[v : v + 1]
            return density

        def project_side(start, density):
            turns = 2 if pn % 4 == 0 else 1

            def step(i, t):
                for turn in range(turns):
                    t = project(lax.rem(start + pn - 2 * (turns * i + turn), pn), t, turn)
                return t

            return lax.fori_loop(0, pn // 2 // turns, step, density)

        density = project_side(me_p, jnp.zeros((nvec, ml), F32))
        if a == 0:
            @pl.loop(0, pn // 2)
            def _(i):
                orb_wait(lax.rem(partner + pn - 2 * i, pn))

            for e in range(2 * pairs):
                val_own[e] = orb_all[dest[e], 0:valence, :]
            val_all[me_v] = val_own[...]
            vert_send(val_own, val_all, (val_sem.at[vn], val_sem.at[me_v]))
        density = project_side(partner, density)
        dens_own[a] = density
        dens_all[a, me_v] = density
        vert_send(dens_own.at[a], dens_all.at[a], (dens_sem.at[0, a], dens_sem.at[1, a]))

        if a == 0:
            scr_copy.wait()
            sibling = me_v + 1 - 2 * lax.rem(me_v, 2)
            order = [lax.rem(side + 2 * j, vn) for j in range(vn // 2) for side in (me_v, sibling)]
            for place, w in enumerate(order):
                if place:
                    drain(val_all.at[w], val_sem.at[w])
                for p in range(pairs):
                    one = val_all[w, 2 * p].astype(F32)
                    two = val_all[w, 2 * p + 1].astype(F32)
                    for v in range(valence):
                        left[p, v * valence : (v + 1) * valence, :] = (one[v : v + 1] * two).astype(BF16)
                for p in range(pairs):
                    matrix = scr[pair_slot[p], pl.ds(pl.multiple_of(w * ml, ml), ml), :]
                    total = jnp.dot(left[p], matrix, preferred_element_type=F32)
                    if place:
                        total = total + half[p]
                    if place == vn - 1:
                        total = total.astype(BF16).astype(F32)
                    half[p] = total

        for p in range(pairs):
            for h in range(ml // LANES):
                cols = slice(h * LANES, (h + 1) * LANES)
                ahead = [proj[dest[2 * p + 1], u * nvec : (u + 1) * nvec, cols] for u in range(valence)]

                def contract(v, other, p=p, cols=cols, ahead=ahead):
                    here = pl.ds(pl.multiple_of(v * nvec, nvec), nvec)
                    line = half[p, pl.ds(pl.multiple_of(v * valence, valence), valence), cols]
                    mine = proj[dest[2 * p], here, cols]
                    sums, kept = [], []
                    for u in range(valence):
                        spread = jnp.broadcast_to(line[u : u + 1], (nvec, LANES))
                        sums.append(spread * ahead[u])
                        kept.append(other[u] + spread * mine)
                    while len(sums) > 1:
                        sums = [sum(sums[i : i + 2]) for i in range(0, len(sums), 2)]
                    weighted[2 * p, here, cols] = sums[0]
                    return tuple(kept)

                zero = jnp.zeros((nvec, LANES), F32)
                other = lax.fori_loop(0, valence, contract, (zero,) * valence)
                for u in range(valence):
                    weighted[2 * p + 1, u * nvec : (u + 1) * nvec, cols] = other[u]

        for e in range(2 * pairs):
            result[e] = back(weighted[e], dest[e])

        def assemble(d, own):
            for k in range(kl):
                total = bare_part[k] if own else jnp.zeros((nvec, width), F32)
                for e in range(2 * pairs):
                    total = total - jnp.where(dest[e] == d * kl + k, 1.0, 0.0) * result[e]
                for w in range(vn):
                    for h in range(halves):
                        at = (h * kl + k) * nl
                        part[a, d * vn + w, at : at + nl, :] = total[
                            w * nl : (w + 1) * nl, h * LANES : (h + 1) * LANES]

        def part_send(d, w):
            pltpu.make_async_remote_copy(
                src_ref=part.at[a, d * vn + w], dst_ref=part_all.at[a, me], send_sem=part_sem.at[0, a],
                recv_sem=part_sem.at[1, a], device_id=(d, w), device_id_type=MESH).start()

        @pl.loop(1, pn)
        def _(i):
            d = lax.rem(me_p + i, pn)
            assemble(d, False)

            @pl.loop(0, vn)
            def _(w):
                part_send(d, lax.rem(me_v + w, vn))

        drain(dens_all.at[a, pl.ds(0, vn - 1)], dens_sem.at[1, a])
        if a == 0:
            bare_copy.wait()
        potential = jnp.zeros((nvec, ml), F32)
        for w in range(vn):
            potential = potential + lax.dot_general(
                dens_all[a, w].astype(BF16), bare_own[:, w * ml : (w + 1) * ml], TRANSPOSED,
                preferred_element_type=F32)
        potential = potential.astype(BF16).astype(F32)
        for k in range(kl):
            vals = orb[k, 0:valence, :].astype(F32)
            value = jnp.concatenate([vals[v : v + 1] * potential for v in range(valence)], axis=0)
            bare_part[k] = 2.0 * back(value, me_p * kl + k)
        assemble(me_p, True)

        @pl.loop(1, vn)
        def _(w):
            part_send(me_p, lax.rem(me_v + w, vn))

        part_all[a, me] = part[a, me]
        drain(part_all.at[a, pl.ds(0, count - 1)], part_sem.at[1, a])
        total = jnp.sum(part_all[a], axis=0)
        current = x_own[a].astype(BF16).astype(F32)
        return trans_tile[...] * current + total

    first_step = apply_kernel(0)
    x_own[1] = first_step
    x_send(1)
    second_step = 2.0 * apply_kernel(1) - trial_tile[...]
    filtered = cheb[0] * trial_tile[...] + cheb[1] * x_own[1] + cheb[2] * second_step
    for h in range(halves):
        for k in range(kl):
            for n in range(nl):
                at = (h * kl + k) * nl + n
                out[n, k : k + 1, h * LANES : (h + 1) * LANES] = filtered[at : at + 1]

    drain(orb_all.at[pl.ds(0, (pn - 1) * kl)], orb_sem)
    drain(val_all.at[pl.ds(0, vn - 1)], val_sem.at[vn])
    for a in range(2):
        drain(x_all.at[a, pl.ds(0, count - 1)], x_sem.at[0, a])
        drain(dens_all.at[a, pl.ds(0, vn - 1)], dens_sem.at[0, a])
        drain(part_all.at[a, pl.ds(0, count - 1)], part_sem.at[0, a])


def body(pn, vn, orbitals, transition, trial, screened, bare, cheb, pair_k, pair_slot, k_order):
    kl, bands, ml = orbitals.shape
    nl, _, width = trial.shape
    pairs = pair_k.shape[0]
    ktot = k_order.shape[0]
    nvec = nl * vn
    count = pn * vn
    tile = (nl * kl * width // LANES, LANES)
    vmem = pl.BlockSpec(memory_space=pltpu.VMEM)
    smem = pl.BlockSpec(memory_space=pltpu.SMEM)
    dma = pltpu.SemaphoreType.DMA
    return pl.pallas_call(
        functools.partial(kernel, pn, vn),
        out_shape=jax.ShapeDtypeStruct(trial.shape, F32),
        in_specs=[vmem, vmem, vmem] + [pl.BlockSpec(memory_space=pl.ANY)] * 2 + [smem, smem, smem, smem],
        out_specs=vmem,
        scratch_shapes=[
            pltpu.VMEM((ktot, bands, ml), BF16),
            pltpu.VMEM((2, count) + tile, F32),
            pltpu.VMEM((2,) + tile, F32),
            pltpu.VMEM((2 * kl, nvec, width), F32),
            pltpu.VMEM(tile, F32),
            pltpu.VMEM(tile, F32),
            pltpu.VMEM((ktot, NV * nvec, ml), F32),
            pltpu.VMEM((2 * pairs, NV, ml), BF16),
            pltpu.VMEM((vn, 2 * pairs, NV, ml), BF16),
            pltpu.VMEM((pairs, NV * NV, ml), BF16),
            pltpu.VMEM((pairs, NV * NV, ml), F32),
            pltpu.VMEM(screened.shape, BF16),
            pltpu.VMEM((2, nvec, ml), F32),
            pltpu.VMEM((2, vn, nvec, ml), F32),
            pltpu.VMEM((ml, vn * ml), BF16),
            pltpu.VMEM((2 * pairs, NV * nvec, ml), F32),
            pltpu.VMEM((2 * pairs, nvec, width), F32),
            pltpu.VMEM((kl, nvec, width), F32),
            pltpu.VMEM((2, count) + tile, F32),
            pltpu.VMEM((2, count) + tile, F32),
            dma, dma, dma, dma((pn,)), dma((vn + 1,)), dma((2, 2)), dma((2, 2)), dma((2, 2)),
        ],
        compiler_params=pltpu.CompilerParams(
            collective_id=0, has_side_effects=True, vmem_limit_bytes=56 * 2**20),
    )(orbitals, transition, trial, screened, bare, cheb, pair_k, pair_slot, k_order)


def solution(mesh):
    in_specs = (
        P("pb", None, "vert"),
        P("pb", None),
        P("vert", "pb", None),
        P("pb", None, "vert"),
        P(),
        P(),
        P("pb"),
        P("pb"),
        P(),
    )
    out_specs = P("vert", "pb", None)
    step = functools.partial(body, mesh.shape["pb"], mesh.shape["vert"])
    return jax.shard_map(step, mesh=mesh, in_specs=in_specs, out_specs=out_specs, check_vma=False)
```
